32 devices in a mesh: ctx: 8 (over y, x, core), tp: 4 (over z).
Axes of the slice: x: 2, y: 2, z: 4, core: 2. Of those that a mesh axis runs over, the one named last changes fastest.
Arguments:
- inputs: bfloat16 [8192, 4096], P('ctx'), may hold values from -6 to 6
- queries: bfloat16 [8192, 4096], P('ctx', 'tp'), may hold values from -6 to 6
- kv_weight: bfloat16 [4096, 2, 4096], P(None, None, 'tp'), may hold values from -0.09375 to 0.09375
- short_taps: float32 [3, 2, 4096], P(None, None, 'tp'), may hold values from -3 to 3
- filter_taps: bfloat16 [8192, 4096], P('ctx', 'tp'), may hold values from -4 to 4
- skip_gain: float32 [4096], P('tp'), may hold values from 0.5 to 1.5
- out_weight: bfloat16 [4096, 4096], P('tp'), may hold values from -0.09375 to 0.09375
Outputs:
- mixed: bfloat16 [8192, 4096], P(('ctx', 'tp'))
The draws below stay inside these ranges and needn't reach their ends.
All inputs are finite; a program needn't handle non-finite values.
Results may differ from the reference program's by a relative error of at most 0.015.
Values may be sent and summed in bfloat16 or wider, within the bound.
A program may use at most 320 MiB of HBM per device.

```python
import jax
import jax.numpy as jnp
from jax import lax

D = 4096
TOKENS = 8192
N_TP = 4


def draw_filter_taps(key, part):
    key_rate, key_kind, key_noise = jax.random.split(key, 3)
    length = TOKENS
    kinds = jax.random.randint(key_kind, (D,), 0, 2)
    slow_mask = kinds > 0
    unit = jax.random.uniform(key_rate, (D,), jnp.float32)
    slow_rate = jnp.exp(jnp.log(0.25 / length) + unit * jnp.log(4.0))
    fast_rate = jnp.exp(jnp.log(1.0 / 50.0) + unit * jnp.log(50.0 / 30.0))
    rates = jnp.where(slow_mask, slow_rate, fast_rate)
    positions = jnp.arange(length, dtype=jnp.float32)[:, None]
    envelope = jnp.exp(-rates[None, :] * positions)
    scaling = jnp.sqrt(2.0 * rates / (1.0 - jnp.exp(-2.0 * rates * length)))
    noise = jax.random.normal(key_noise, (length, D), jnp.float32)
    return (noise * envelope * scaling[None, :]).astype(jnp.bfloat16)


def block_levels(stream_key, extent, cuts, least, top_value):
    def one(dim, parts):
        steps = jax.random.uniform(jax.random.fold_in(jax.random.fold_in(stream_key, 6), dim), (parts,), jnp.float32, least / len(cuts), top_value / len(cuts))
        return jnp.repeat(jnp.exp(steps), extent[dim] // parts).reshape((-1,) + (1,) * (len(extent) - dim - 1))

    level = one(*cuts[0])
    for cut in cuts[1:]:
        level = level * one(*cut)
    return level


def centred(stream_key, dims, spread, bound, cuts=(), held_as=jnp.bfloat16):
    loudness = block_levels(stream_key, dims, cuts, -0.22, 0.18) if cuts else 1.0
    drawn = jax.random.normal(stream_key, dims, jnp.float32) * spread * loudness
    return jnp.minimum(jnp.maximum(drawn, -bound), bound).astype(held_as)


def setup_inputs(seed: int = 0) -> dict:
    arg_keys = jax.random.split(jax.random.key(seed), 8)
    return {
        "inputs": centred(arg_keys[0], (TOKENS, D), 1.0, 6.0, ((0, 8),)),
        "queries": centred(arg_keys[1], (TOKENS, D), 1.0, 6.0, ((0, 8), (1, 4))),
        "kv_weight": centred(arg_keys[2], (D, 2, D), D ** -0.5, 0.09375, ((2, 4),)),
        "short_taps": centred(arg_keys[3], (3, 2, D), 0.6, 3.0, ((2, 4),), jnp.float32),
        "filter_taps": draw_filter_taps(jax.random.fold_in(arg_keys[7], 71), 0),
        "skip_gain": jnp.clip(0.5 + 1.0 * jax.random.uniform(arg_keys[5], (D,), jnp.float32) ** block_levels(arg_keys[5], (D,), ((0, 4),), -0.2, 0.2), 0.5, 1.5),
        "out_weight": centred(arg_keys[6], (D, D), D ** -0.5, 0.09375, ((0, 4),)),
    }


def causal_conv(signal, taps):
    padded = 2 * signal.shape[0]
    spec_sig = jnp.fft.rfft(signal, n=padded, axis=0)
    spec_tap = jnp.fft.rfft(taps, n=padded, axis=0)
    return jnp.fft.irfft(spec_sig * spec_tap, n=padded, axis=0)[: signal.shape[0]]


def reference(inputs, queries, kv_weight, short_taps, filter_taps, skip_gain, out_weight):
    width = D // N_TP
    length = inputs.shape[0]
    inputs_wide = inputs.astype(jnp.float32)

    def group_step(accum, index):
        start = (index * width).astype(jnp.int32)
        weight_cols = lax.dynamic_slice_in_dim(kv_weight, start, width, 2).astype(jnp.float32)
        projected = jnp.einsum("td,dkc->tkc", inputs_wide, weight_cols).astype(jnp.bfloat16)
        taps_three = lax.dynamic_slice_in_dim(short_taps, start, width, 2)
        extended = jnp.concatenate([jnp.zeros((2, 2, width), jnp.float32), projected.astype(jnp.float32)], 0)
        smoothed = taps_three[0] * extended[2:] + taps_three[1] * extended[1:-1] + taps_three[2] * extended[:-2]
        kv_product = (smoothed[:, 0] * smoothed[:, 1]).astype(jnp.bfloat16)
        kv_wide = kv_product.astype(jnp.float32)
        long_taps = lax.dynamic_slice_in_dim(filter_taps, start, width, 1).astype(jnp.float32)
        long_conv = causal_conv(kv_wide, long_taps)
        query_cols = lax.dynamic_slice_in_dim(queries, start, width, 1).astype(jnp.float32)
        gain_cols = lax.dynamic_slice_in_dim(skip_gain, start, width, 0)
        gated = (query_cols * (long_conv + gain_cols[None, :] * kv_wide)).astype(jnp.bfloat16)
        out_rows = lax.dynamic_slice_in_dim(out_weight, start, width, 0)
        partial_g = jnp.dot(gated, out_rows, preferred_element_type=jnp.float32).astype(jnp.bfloat16)
        return accum + partial_g.astype(jnp.float32), None

    accum, _ = lax.scan(group_step, jnp.zeros((length, D), jnp.float32), jnp.arange(N_TP, dtype=jnp.int32))
    return accum.astype(jnp.bfloat16)
```

```python
import functools

import jax
import jax.numpy as jnp
import ml_dtypes
import numpy as np
from jax import lax
from jax.experimental import pallas as pl
from jax.experimental.pallas import tpu as pltpu
from jax.sharding import PartitionSpec as P

SECOND = 128
SUB = 8


def shifted(value, axis, steps):
    count = lax.axis_size(axis)
    leading, last = (max(0, -steps), min(count, count - steps))
    return lax.ppermute(value, axis, [(source, source + steps) for source in range(leading, last)])


@functools.lru_cache(maxsize=None)
def tables(length):
    padded = 2 * length
    outer = padded // SECOND
    used = outer // 2
    half = outer // 2 + 1
    k1 = np.arange(half)
    head_angle = 2.0 * np.pi / outer * (k1[:, None] * np.arange(used)[None, :] % outer)
    head = np.stack([np.cos(head_angle), -np.sin(head_angle)], 1).reshape(2 * half, used)
    spread = np.zeros((2 * half, SUB, used, SUB), np.float32)
    for s in range(SUB):
        spread[:, s, :, s] = head
    first = spread.reshape(2 * half * SUB, used * SUB)
    q = np.arange(SECOND)
    freq = k1[:, None] + outer * np.arange(SECOND)[None, :]
    angle = 2.0 * np.pi / padded * (freq[:, :, None] * q[None, None, :] % padded)
    cos_t, sin_t = np.cos(angle).astype(np.float32), -np.sin(angle).astype(np.float32)
    mid = np.concatenate(
        [np.concatenate([cos_t, -sin_t], 2), np.concatenate([sin_t, cos_t], 2)], 1
    )
    narrow = lambda t: np.ascontiguousarray(t).astype(ml_dtypes.bfloat16)
    return narrow(first), narrow(first.T), narrow(mid), narrow(mid.transpose(0, 2, 1))


def conv_kernel(
    half, per_step, scale, kv_ref, taps_ref, first_ref, last_ref, fwd_ref, inv_ref, out_ref, a_ref, b_ref
):
    used = kv_ref.shape[0]
    channels = kv_ref.shape[2]
    step = pl.program_id(0)
    f32 = jnp.float32

    @pl.when(step == 0)
    def _():
        @pl.loop(0, SECOND // 16)
        def _(block):
            rows = pl.ds(pl.multiple_of(block * 16, 16), 16)
            data = jnp.concatenate([kv_ref[:, rows, :], taps_ref[:, rows, :]], axis=2).astype(f32)
            for part in range(2):
                piece = data[:, part * SUB : (part + 1) * SUB, :]
                piece = piece.reshape(used * SUB, 2 * channels).astype(jnp.bfloat16)
                got = jnp.dot(first_ref[...], piece, preferred_element_type=f32)
                into = pl.ds(pl.multiple_of(block * 16 + part * SUB, SUB), SUB)
                a_ref[:, into, :] = got.reshape(2 * half, SUB, 2 * channels)

    for j in range(per_step):
        k1 = step * per_step + j
        pair = pl.ds(2 * k1, 2)
        turned = a_ref[pair].reshape(2 * SECOND, 2 * channels).astype(jnp.bfloat16)
        spec = jnp.dot(fwd_ref[j], turned, preferred_element_type=f32)
        sig_r, sig_i = spec[:SECOND, :channels], spec[SECOND:, :channels]
        tap_r, tap_i = spec[:SECOND, channels:], spec[SECOND:, channels:]
        weight = jnp.where((k1 == 0) | (k1 == half - 1), scale, 2.0 * scale).astype(f32)
        tap_r, tap_i = tap_r * weight, tap_i * weight
        prod_r = sig_r * tap_r - sig_i * tap_i
        prod_i = sig_r * tap_i + sig_i * tap_r
        prod = jnp.concatenate([prod_r, prod_i], 0).astype(jnp.bfloat16)
        back = jnp.dot(inv_ref[j], prod, preferred_element_type=f32)
        b_ref[pair] = back.reshape(2, SECOND, channels)

    @pl.when(step == pl.num_programs(0) - 1)
    def _():
        @pl.loop(0, SECOND // 16)
        def _(block):
            pieces = []
            for part in range(2):
                rows = pl.ds(pl.multiple_of(block * 16 + part * SUB, SUB), SUB)
                piece = b_ref[:, rows, :].reshape(2 * half * SUB, channels).astype(jnp.bfloat16)
                got = jnp.dot(last_ref[...], piece, preferred_element_type=f32)
                pieces.append(got.reshape(used, SUB, channels))
            into = pl.ds(pl.multiple_of(block * 16, 16), 16)
            out_ref[:, into, :] = jnp.concatenate(pieces, axis=1).astype(out_ref.dtype)


def local_conv(kv, taps):
    length, channels = kv.shape
    first, last, fwd, inv = tables(length)
    used = length // SECOND
    half = fwd.shape[0]
    per_step = max(n for n in range(1, 6) if half % n == 0)
    shape = (used, SECOND, channels)
    whole = lambda *dims: pl.BlockSpec(dims, lambda i: (0,) * len(dims), pipeline_mode=pl.Buffered(1))
    table = pl.BlockSpec((per_step, 2 * SECOND, 2 * SECOND), lambda i: (i, 0, 0))
    out = pl.pallas_call(
        functools.partial(conv_kernel, half, per_step, 0.5 / length),
        grid=(half // per_step,),
        out_shape=jax.ShapeDtypeStruct(shape, jnp.bfloat16),
        in_specs=[whole(*shape), whole(*shape), whole(*first.shape), whole(*last.shape), table, table],
        out_specs=whole(*shape),
        scratch_shapes=[
            pltpu.VMEM((2 * half, SECOND, 2 * channels), jnp.float32),
            pltpu.VMEM((2 * half, SECOND, channels), jnp.float32),
        ],
        compiler_params=pltpu.CompilerParams(vmem_limit_bytes=60 * 2**20),
    )(kv.reshape(shape), taps.reshape(shape), first, last, fwd, inv)
    return out.reshape(length, channels)


def body(inputs, queries, kv_weight, short_taps, filter_taps, skip_gain, out_weight):
    taps_all = lax.all_to_all(filter_taps, "ctx", split_axis=1, concat_axis=0, tiled=True)
    projected = jnp.einsum(
        "td,dkc->tkc", inputs, kv_weight, preferred_element_type=jnp.float32
    ).astype(jnp.bfloat16)
    carried = shifted(projected[-2:], "ctx", 1)
    extended = jnp.concatenate([carried, projected], 0).astype(jnp.float32)
    smoothed = (
        short_taps[0] * extended[2:]
        + short_taps[1] * extended[1:-1]
        + short_taps[2] * extended[:-2]
    )
    kv_product = (smoothed[:, 0] * smoothed[:, 1]).astype(jnp.bfloat16)
    kv_all = lax.all_to_all(kv_product, "ctx", split_axis=1, concat_axis=0, tiled=True)
    conv_all = local_conv(kv_all, taps_all)
    long_conv = lax.all_to_all(conv_all, "ctx", split_axis=0, concat_axis=1, tiled=True)
    gated = (
        queries.astype(jnp.float32)
        * (long_conv.astype(jnp.float32) + skip_gain[None, :] * kv_product.astype(jnp.float32))
    ).astype(jnp.bfloat16)
    return lax.psum_scatter(
        jnp.dot(gated, out_weight, preferred_element_type=jnp.float32).astype(jnp.bfloat16),
        "tp",
        scatter_dimension=0,
        tiled=True,
    )


def solution(mesh):
    return jax.shard_map(
        body,
        mesh=mesh,
        in_specs=(
            P("ctx", None),
            P("ctx", "tp"),
            P(None, None, "tp"),
            P(None, None, "tp"),
            P("ctx", "tp"),
            P("tp"),
            P("tp", None),
        ),
        out_specs=P(("ctx", "tp"), None),
        check_vma=False,
    )
```

```python
import functools

import jax
import jax.numpy as jnp
import ml_dtypes
import numpy as np
from jax import lax
from jax.experimental import pallas as pl
from jax.experimental.pallas import tpu as pltpu
from jax.sharding import PartitionSpec as P

SECOND = 128
SUB = 8


def shifted(value, axis, steps):
    count = lax.axis_size(axis)
    leading, last = (max(0, -steps), min(count, count - steps))
    return lax.ppermute(value, axis, [(source, source + steps) for source in range(leading, last)])


@functools.lru_cache(maxsize=None)
def tables(length):
    padded = 2 * length
    outer = padded // SECOND
    used = outer // 2
    half = outer // 2 + 1
    k1 = np.arange(half)
    head_angle = 2.0 * np.pi / outer * (k1[:, None] * np.arange(used)[None, :] % outer)
    head = np.stack([np.cos(head_angle), -np.sin(head_angle)], 1).reshape(2 * half, used)
    spread = np.zeros((2 * half, SUB, used, SUB), np.float32)
    for s in range(SUB):
        spread[:, s, :, s] = head
    first = spread.reshape(2 * half * SUB, used * SUB)
    q = np.arange(SECOND)
    freq = k1[:, None] + outer * np.arange(SECOND)[None, :]
    angle = 2.0 * np.pi / padded * (freq[:, :, None] * q[None, None, :] % padded)
    cos_t, sin_t = np.cos(angle).astype(np.float32), -np.sin(angle).astype(np.float32)
    mid = np.concatenate(
        [np.concatenate([cos_t, -sin_t], 2), np.concatenate([sin_t, cos_t], 2)], 1
    )
    narrow = lambda t: np.ascontiguousarray(t).astype(ml_dtypes.bfloat16)
    return narrow(first), narrow(first.T), narrow(mid), narrow(mid.transpose(0, 2, 1))


def conv_kernel(
    half, per_step, scale, kv_ref, taps_ref, first_ref, last_ref, fwd_ref, inv_ref, out_ref, a_ref, b_ref
):
    used = kv_ref.shape[0]
    channels = kv_ref.shape[2]
    step = pl.program_id(0)
    f32 = jnp.float32

    @pl.when(step == 0)
    def _():
        @pl.loop(0, SECOND // 16)
        def _(block):
            rows = pl.ds(pl.multiple_of(block * 16, 16), 16)
            data = jnp.concatenate([kv_ref[:, rows, :], taps_ref[:, rows, :]], axis=2).astype(f32)
            for part in range(2):
                piece = data[:, part * SUB : (part + 1) * SUB, :]
                piece = piece.reshape(used * SUB, 2 * channels).astype(jnp.bfloat16)
                got = jnp.dot(first_ref[...], piece, preferred_element_type=f32)
                into = pl.ds(pl.multiple_of(block * 16 + part * SUB, SUB), SUB)
                a_ref[:, into, :] = got.reshape(2 * half, SUB, 2 * channels)

    for j in range(per_step):
        k1 = step * per_step + j
        pair = pl.ds(2 * k1, 2)
        turned = a_ref[pair].reshape(2 * SECOND, 2 * channels).astype(jnp.bfloat16)
        spec = jnp.dot(fwd_ref[j], turned, preferred_element_type=f32)
        sig_r, sig_i = spec[:SECOND, :channels], spec[SECOND:, :channels]
        tap_r, tap_i = spec[:SECOND, channels:], spec[SECOND:, channels:]
        weight = jnp.where((k1 == 0) | (k1 == half - 1), scale, 2.0 * scale).astype(f32)
        tap_r, tap_i = tap_r * weight, tap_i * weight
        prod_r = sig_r * tap_r - sig_i * tap_i
        prod_i = sig_r * tap_i + sig_i * tap_r
        prod = jnp.concatenate([prod_r, prod_i], 0).astype(jnp.bfloat16)
        back = jnp.dot(inv_ref[j], prod, preferred_element_type=f32)
        b_ref[pair] = back.reshape(2, SECOND, channels)

    @pl.when(step == pl.num_programs(0) - 1)
    def _():
        @pl.loop(0, SECOND // 16)
        def _(block):
            pieces = []
            for part in range(2):
                rows = pl.ds(pl.multiple_of(block * 16 + part * SUB, SUB), SUB)
                piece = b_ref[:, rows, :].reshape(2 * half * SUB, channels).astype(jnp.bfloat16)
                got = jnp.dot(last_ref[...], piece, preferred_element_type=f32)
                pieces.append(got.reshape(used, SUB, channels))
            into = pl.ds(pl.multiple_of(block * 16, 16), 16)
            out_ref[:, into, :] = jnp.concatenate(pieces, axis=1).astype(out_ref.dtype)


def local_conv(kv, taps):
    length, channels = kv.shape
    first, last, fwd, inv = tables(length)
    used = length // SECOND
    half = fwd.shape[0]
    per_step = max(n for n in range(1, 6) if half % n == 0)
    shape = (used, SECOND, channels)
    whole = lambda *dims: pl.BlockSpec(dims, lambda i: (0,) * len(dims), pipeline_mode=pl.Buffered(1))
    table = pl.BlockSpec((per_step, 2 * SECOND, 2 * SECOND), lambda i: (i, 0, 0))
    out = pl.pallas_call(
        functools.partial(conv_kernel, half, per_step, 0.5 / length),
        grid=(half // per_step,),
        out_shape=jax.ShapeDtypeStruct(shape, jnp.bfloat16),
        in_specs=[whole(*shape), whole(*shape), whole(*first.shape), whole(*last.shape), table, table],
        out_specs=whole(*shape),
        scratch_shapes=[
            pltpu.VMEM((2 * half, SECOND, 2 * channels), jnp.float32),
            pltpu.VMEM((2 * half, SECOND, channels), jnp.float32),
        ],
        compiler_params=pltpu.CompilerParams(vmem_limit_bytes=60 * 2**20),
    )(kv.reshape(shape), taps.reshape(shape), first, last, fwd, inv)
    return out.reshape(length, channels)


def body(inputs, queries, kv_weight, short_taps, filter_taps, skip_gain, out_weight):
    groups, shards = lax.axis_size("tp"), lax.axis_size("ctx")
    group, core = lax.axis_index("tp"), lax.axis_index("ctx") % 2
    mates = [(d, d ^ 1) for d in range(groups)]
    siblings = [(d, d ^ 1) for d in range(shards)]
    half_rows = out_weight.shape[0] // 2
    part_rows = half_rows // 2
    fetched = [
        lax.ppermute(
            lax.dynamic_slice_in_dim(out_weight, core * half_rows + j * part_rows, part_rows, 0),
            "tp",
            mates,
        )
        for j in range(2)
    ]
    taps_all = lax.all_to_all(filter_taps, "ctx", split_axis=1, concat_axis=0, tiled=True)
    projected = jnp.einsum(
        "td,dkc->tkc", inputs, kv_weight, preferred_element_type=jnp.float32
    ).astype(jnp.bfloat16)
    projected, taps_all = lax.optimization_barrier((projected, taps_all))
    carried = shifted(projected[-2:], "ctx", 1)
    extended = jnp.concatenate([carried, projected], 0).astype(jnp.float32)
    smoothed = (
        short_taps[0] * extended[2:]
        + short_taps[1] * extended[1:-1]
        + short_taps[2] * extended[:-2]
    )
    kv_product = (smoothed[:, 0] * smoothed[:, 1]).astype(jnp.bfloat16)
    kv_all = lax.all_to_all(kv_product, "ctx", split_axis=1, concat_axis=0, tiled=True)
    kv_all, fetched[0] = lax.optimization_barrier((kv_all, fetched[0]))
    conv_all = local_conv(kv_all, taps_all)
    conv_all, fetched[1] = lax.optimization_barrier((conv_all, fetched[1]))
    passed = [lax.ppermute(part, "ctx", siblings) for part in fetched]
    long_conv = lax.all_to_all(conv_all, "ctx", split_axis=0, concat_axis=1, tiled=True)
    gated = (
        queries.astype(jnp.float32)
        * (long_conv.astype(jnp.float32) + skip_gain[None, :] * kv_product.astype(jnp.float32))
    ).astype(jnp.bfloat16)
    mate_weight = jnp.concatenate(fetched + passed, 0)
    turned = jnp.where(
        core == 0, gated, jnp.concatenate([gated[:, half_rows:], gated[:, :half_rows]], 1)
    )
    rows = gated.shape[0] // groups

    def chunk(array, index):
        return lax.dynamic_slice_in_dim(array, index % groups * rows, rows, 0)

    steps = list(range(2, groups, 2)) + [0]
    received = {
        step: lax.ppermute(chunk(turned, (group ^ 1) + step), "tp", mates) for step in steps
    }
    arrived = []
    for step in steps:
        part = jnp.dot(
            chunk(gated, group + step), out_weight, preferred_element_type=jnp.float32
        ) + jnp.dot(received[step], mate_weight, preferred_element_type=jnp.float32)
        if step:
            ring = [(d, (d + step) % groups) for d in range(groups)]
            arrived.append(lax.ppermute(part.astype(jnp.bfloat16), "tp", ring))
    for other in arrived:
        part = part + other.astype(jnp.float32)
    return part.astype(jnp.bfloat16)


def solution(mesh):
    return jax.shard_map(
        body,
        mesh=mesh,
        in_specs=(
            P("ctx", None),
            P("ctx", "tp"),
            P(None, None, "tp"),
            P(None, None, "tp"),
            P("ctx", "tp"),
            P("tp"),
            P("tp", None),
        ),
        out_specs=P(("ctx", "tp"), None),
        check_vma=False,
    )
```

```python
import functools

import jax
import jax.numpy as jnp
import ml_dtypes
import numpy as np
from jax import lax
from jax.experimental import pallas as pl
from jax.experimental.pallas import tpu as pltpu
from jax.sharding import PartitionSpec as P

SECOND = 128
SUB = 8


def shifted(value, axis, steps):
    count = lax.axis_size(axis)
    leading, last = (max(0, -steps), min(count, count - steps))
    return lax.ppermute(value, axis, [(source, source + steps) for source in range(leading, last)])


@functools.lru_cache(maxsize=None)
def tables(length):
    padded = 2 * length
    outer = padded // SECOND
    used = outer // 2
    half = outer // 2 + 1
    k1 = np.arange(half)
    head_angle = 2.0 * np.pi / outer * (k1[:, None] * np.arange(used)[None, :] % outer)
    head = np.stack([np.cos(head_angle), -np.sin(head_angle)], 1).reshape(2 * half, used)
    spread = np.zeros((2 * half, SUB, used, SUB), np.float32)
    for s in range(SUB):
        spread[:, s, :, s] = head
    first = spread.reshape(2 * half * SUB, used * SUB)
    q = np.arange(SECOND)
    freq = k1[:, None] + outer * np.arange(SECOND)[None, :]
    angle = 2.0 * np.pi / padded * (freq[:, :, None] * q[None, None, :] % padded)
    cos_t, sin_t = np.cos(angle).astype(np.float32), -np.sin(angle).astype(np.float32)
    mid = np.concatenate(
        [np.concatenate([cos_t, -sin_t], 2), np.concatenate([sin_t, cos_t], 2)], 1
    )
    narrow = lambda t: np.ascontiguousarray(t).astype(ml_dtypes.bfloat16)
    return narrow(first), narrow(first.T), narrow(mid), narrow(mid.transpose(0, 2, 1))


def conv_kernel(
    half, per_step, scale, kv_ref, taps_ref, first_ref, last_ref, fwd_ref, inv_ref, out_ref, a_ref, b_ref
):
    used = kv_ref.shape[0]
    channels = kv_ref.shape[2]
    step = pl.program_id(0)
    f32 = jnp.float32

    @pl.when(step == 0)
    def _():
        @pl.loop(0, SECOND // 16)
        def _(block):
            rows = pl.ds(pl.multiple_of(block * 16, 16), 16)
            data = jnp.concatenate([kv_ref[:, rows, :], taps_ref[:, rows, :]], axis=2).astype(f32)
            for part in range(2):
                piece = data[:, part * SUB : (part + 1) * SUB, :]
                piece = piece.reshape(used * SUB, 2 * channels).astype(jnp.bfloat16)
                got = jnp.dot(first_ref[...], piece, preferred_element_type=f32)
                into = pl.ds(pl.multiple_of(block * 16 + part * SUB, SUB), SUB)
                a_ref[:, into, :] = got.reshape(2 * half, SUB, 2 * channels)

    for j in range(per_step):
        k1 = step * per_step + j
        pair = pl.ds(2 * k1, 2)
        turned = a_ref[pair].reshape(2 * SECOND, 2 * channels).astype(jnp.bfloat16)
        spec = jnp.dot(fwd_ref[j], turned, preferred_element_type=f32)
        sig_r, sig_i = spec[:SECOND, :channels], spec[SECOND:, :channels]
        tap_r, tap_i = spec[:SECOND, channels:], spec[SECOND:, channels:]
        weight = jnp.where((k1 == 0) | (k1 == half - 1), scale, 2.0 * scale).astype(f32)
        tap_r, tap_i = tap_r * weight, tap_i * weight
        prod_r = sig_r * tap_r - sig_i * tap_i
        prod_i = sig_r * tap_i + sig_i * tap_r
        prod = jnp.concatenate([prod_r, prod_i], 0).astype(jnp.bfloat16)
        back = jnp.dot(inv_ref[j], prod, preferred_element_type=f32)
        b_ref[pair] = back.reshape(2, SECOND, channels)

    @pl.when(step == pl.num_programs(0) - 1)
    def _():
        @pl.loop(0, SECOND // 16)
        def _(block):
            pieces = []
            for part in range(2):
                rows = pl.ds(pl.multiple_of(block * 16 + part * SUB, SUB), SUB)
                piece = b_ref[:, rows, :].reshape(2 * half * SUB, channels).astype(jnp.bfloat16)
                got = jnp.dot(last_ref[...], piece, preferred_element_type=f32)
                pieces.append(got.reshape(used, SUB, channels))
            into = pl.ds(pl.multiple_of(block * 16, 16), 16)
            out_ref[:, into, :] = jnp.concatenate(pieces, axis=1).astype(out_ref.dtype)


def local_conv(kv, taps):
    length, channels = kv.shape
    first, last, fwd, inv = tables(length)
    used = length // SECOND
    half = fwd.shape[0]
    per_step = max(n for n in range(1, 6) if half % n == 0)
    shape = (used, SECOND, channels)
    whole = lambda *dims: pl.BlockSpec(dims, lambda i: (0,) * len(dims), pipeline_mode=pl.Buffered(1))
    table = pl.BlockSpec((per_step, 2 * SECOND, 2 * SECOND), lambda i: (i, 0, 0))
    out = pl.pallas_call(
        functools.partial(conv_kernel, half, per_step, 0.5 / length),
        grid=(half // per_step,),
        out_shape=jax.ShapeDtypeStruct(shape, jnp.bfloat16),
        in_specs=[whole(*shape), whole(*shape), whole(*first.shape), whole(*last.shape), table, table],
        out_specs=whole(*shape),
        scratch_shapes=[
            pltpu.VMEM((2 * half, SECOND, 2 * channels), jnp.float32),
            pltpu.VMEM((2 * half, SECOND, channels), jnp.float32),
        ],
        compiler_params=pltpu.CompilerParams(vmem_limit_bytes=60 * 2**20),
    )(kv.reshape(shape), taps.reshape(shape), first, last, fwd, inv)
    return out.reshape(length, channels)


def body(inputs, queries, kv_weight, short_taps, filter_taps, skip_gain, out_weight):
    groups, shards = lax.axis_size("tp"), lax.axis_size("ctx")
    group, core = lax.axis_index("tp"), lax.axis_index("ctx") % 2
    mates = [(d, d ^ 1) for d in range(groups)]
    siblings = [(d, d ^ 1) for d in range(shards)]
    half_rows = out_weight.shape[0] // 2
    part_rows = half_rows // 2
    fetched = [
        lax.ppermute(
            lax.dynamic_slice_in_dim(out_weight, core * half_rows + j * part_rows, part_rows, 0),
            "tp",
            mates,
        )
        for j in range(2)
    ]
    taps_all = lax.all_to_all(filter_taps, "ctx", split_axis=1, concat_axis=0, tiled=True)
    projected = jnp.einsum(
        "td,dkc->tkc", inputs, kv_weight, preferred_element_type=jnp.float32
    ).astype(jnp.bfloat16)
    projected, taps_all = lax.optimization_barrier((projected, taps_all))
    carried = shifted(projected[-2:], "ctx", 1)
    extended = jnp.concatenate([carried, projected], 0).astype(jnp.float32)
    smoothed = (
        short_taps[0] * extended[2:]
        + short_taps[1] * extended[1:-1]
        + short_taps[2] * extended[:-2]
    )
    kv_product = (smoothed[:, 0] * smoothed[:, 1]).astype(jnp.bfloat16)
    kv_all = lax.all_to_all(kv_product, "ctx", split_axis=1, concat_axis=0, tiled=True)
    kv_all, fetched[0] = lax.optimization_barrier((kv_all, fetched[0]))
    conv_all = local_conv(kv_all, taps_all)
    conv_all, fetched[1] = lax.optimization_barrier((conv_all, fetched[1]))
    passed = [lax.ppermute(part, "ctx", siblings) for part in fetched]
    mate_weight = jnp.concatenate(fetched + passed, 0)
    channels = conv_all.shape[1]
    rows = queries.shape[0] // groups
    conv_all = conv_all.reshape(shards, groups * rows, channels)
    side = group % 2

    def pair_rows(array, step, dim):
        start = (group - side + step) % groups * rows
        return lax.dynamic_slice_in_dim(array, start, 2 * rows, dim)

    def pair_sum(conv_part, step):
        conv_part = conv_part.reshape(shards * 2 * rows, channels)
        long_conv = lax.all_to_all(conv_part, "ctx", split_axis=0, concat_axis=1, tiled=True)
        gated = (
            pair_rows(queries, step, 0).astype(jnp.float32)
            * (
                long_conv.astype(jnp.float32)
                + skip_gain[None, :] * pair_rows(kv_product, step, 0).astype(jnp.float32)
            )
        ).astype(jnp.bfloat16)
        sent = lax.dynamic_slice_in_dim(gated, (1 - side) * rows, rows, 0)
        sent = jnp.where(
            core == 0, sent, jnp.concatenate([sent[:, half_rows:], sent[:, :half_rows]], 1)
        )
        received = lax.ppermute(sent, "tp", mates)
        own = lax.dynamic_slice_in_dim(gated, side * rows, rows, 0)
        return jnp.dot(own, out_weight, preferred_element_type=jnp.float32) + jnp.dot(
            received, mate_weight, preferred_element_type=jnp.float32
        )

    arrived = []
    for step in range(2, groups, 2):
        part = pair_sum(pair_rows(conv_all, step, 1), step).astype(jnp.bfloat16)
        part, conv_all = lax.optimization_barrier((part, conv_all))
        ring = [(d, (d + step) % groups) for d in range(groups)]
        arrived.append(lax.ppermute(part, "tp", ring))
    total = pair_sum(pair_rows(conv_all, 0, 1), 0)
    total, *arrived = lax.optimization_barrier((total, *arrived))
    for other in arrived:
        total = total + other.astype(jnp.float32)
    return total.astype(jnp.bfloat16)


def solution(mesh):
    return jax.shard_map(
        body,
        mesh=mesh,
        in_specs=(
            P("ctx", None),
            P("ctx", "tp"),
            P(None, None, "tp"),
            P(None, None, "tp"),
            P("ctx", "tp"),
            P("tp"),
            P("tp", None),
        ),
        out_specs=P(("ctx", "tp"), None),
        check_vma=False,
    )
```

```python
import functools

import jax
import jax.numpy as jnp
import ml_dtypes
import numpy as np
from jax import lax
from jax.experimental import pallas as pl
from jax.experimental.pallas import tpu as pltpu
from jax.sharding import PartitionSpec as P

SECOND = 128
SUB = 8


def shifted(value, axis, steps):
    count = lax.axis_size(axis)
    leading, last = (max(0, -steps), min(count, count - steps))
    return lax.ppermute(value, axis, [(source, source + steps) for source in range(leading, last)])


@functools.lru_cache(maxsize=None)
def tables(length):
    padded = 2 * length
    outer = padded // SECOND
    used = outer // 2
    half = outer // 2 + 1
    k1 = np.arange(half)
    head_angle = 2.0 * np.pi / outer * (k1[:, None] * np.arange(used)[None, :] % outer)
    head = np.stack([np.cos(head_angle), -np.sin(head_angle)], 1).reshape(2 * half, used)
    spread = np.zeros((2 * half, SUB, used, SUB), np.float32)
    for s in range(SUB):
        spread[:, s, :, s] = head
    first = spread.reshape(2 * half * SUB, used * SUB)
    q = np.arange(SECOND)
    freq = k1[:, None] + outer * np.arange(SECOND)[None, :]
    angle = 2.0 * np.pi / padded * (freq[:, :, None] * q[None, None, :] % padded)
    cos_t, sin_t = np.cos(angle).astype(np.float32), -np.sin(angle).astype(np.float32)
    mid = np.concatenate(
        [np.concatenate([cos_t, -sin_t], 2), np.concatenate([sin_t, cos_t], 2)], 1
    )
    narrow = lambda t: np.ascontiguousarray(t).astype(ml_dtypes.bfloat16)
    return narrow(first), narrow(first.T), narrow(mid), narrow(mid.transpose(0, 2, 1))


def conv_kernel(
    half, per_step, scale, kv_ref, taps_ref, first_ref, last_ref, fwd_ref, inv_ref, out_ref, a_ref, b_ref
):
    used = kv_ref.shape[0]
    channels = kv_ref.shape[2]
    step = pl.program_id(0)
    f32 = jnp.float32

    @pl.when(step == 0)
    def _():
        @pl.loop(0, SECOND // 16)
        def _(block):
            rows = pl.ds(pl.multiple_of(block * 16, 16), 16)
            data = jnp.concatenate([kv_ref[:, rows, :], taps_ref[:, rows, :]], axis=2).astype(f32)
            for part in range(2):
                piece = data[:, part * SUB : (part + 1) * SUB, :]
                piece = piece.reshape(used * SUB, 2 * channels).astype(jnp.bfloat16)
                got = jnp.dot(first_ref[...], piece, preferred_element_type=f32)
                into = pl.ds(pl.multiple_of(block * 16 + part * SUB, SUB), SUB)
                a_ref[:, into, :] = got.reshape(2 * half, SUB, 2 * channels)

    for j in range(per_step):
        k1 = step * per_step + j
        pair = pl.ds(2 * k1, 2)
        turned = a_ref[pair].reshape(2 * SECOND, 2 * channels).astype(jnp.bfloat16)
        spec = jnp.dot(fwd_ref[j], turned, preferred_element_type=f32)
        sig_r, sig_i = spec[:SECOND, :channels], spec[SECOND:, :channels]
        tap_r, tap_i = spec[:SECOND, channels:], spec[SECOND:, channels:]
        weight = jnp.where((k1 == 0) | (k1 == half - 1), scale, 2.0 * scale).astype(f32)
        tap_r, tap_i = tap_r * weight, tap_i * weight
        prod_r = sig_r * tap_r - sig_i * tap_i
        prod_i = sig_r * tap_i + sig_i * tap_r
        prod = jnp.concatenate([prod_r, prod_i], 0).astype(jnp.bfloat16)
        back = jnp.dot(inv_ref[j], prod, preferred_element_type=f32)
        b_ref[pair] = back.reshape(2, SECOND, channels)

    @pl.when(step == pl.num_programs(0) - 1)
    def _():
        @pl.loop(0, SECOND // 16)
        def _(block):
            pieces = []
            for part in range(2):
                rows = pl.ds(pl.multiple_of(block * 16 + part * SUB, SUB), SUB)
                piece = b_ref[:, rows, :].reshape(2 * half * SUB, channels).astype(jnp.bfloat16)
                got = jnp.dot(last_ref[...], piece, preferred_element_type=f32)
                pieces.append(got.reshape(used, SUB, channels))
            into = pl.ds(pl.multiple_of(block * 16, 16), 16)
            out_ref[:, into, :] = jnp.concatenate(pieces, axis=1).astype(out_ref.dtype)


def local_conv(kv, taps):
    length, channels = kv.shape
    first, last, fwd, inv = tables(length)
    used = length // SECOND
    half = fwd.shape[0]
    per_step = max(n for n in range(1, 6) if half % n == 0)
    shape = (used, SECOND, channels)
    whole = lambda *dims: pl.BlockSpec(dims, lambda i: (0,) * len(dims), pipeline_mode=pl.Buffered(1))
    table = pl.BlockSpec((per_step, 2 * SECOND, 2 * SECOND), lambda i: (i, 0, 0))
    out = pl.pallas_call(
        functools.partial(conv_kernel, half, per_step, 0.5 / length),
        grid=(half // per_step,),
        out_shape=jax.ShapeDtypeStruct(shape, jnp.bfloat16),
        in_specs=[whole(*shape), whole(*shape), whole(*first.shape), whole(*last.shape), table, table],
        out_specs=whole(*shape),
        scratch_shapes=[
            pltpu.VMEM((2 * half, SECOND, 2 * channels), jnp.float32),
            pltpu.VMEM((2 * half, SECOND, channels), jnp.float32),
        ],
        compiler_params=pltpu.CompilerParams(vmem_limit_bytes=60 * 2**20),
    )(kv.reshape(shape), taps.reshape(shape), first, last, fwd, inv)
    return out.reshape(length, channels)


def to_channels(block):
    shards = lax.axis_size("ctx")
    length, channels = block.shape
    by_owner = block.reshape(length, shards, channels // shards).transpose(1, 0, 2)
    moved = lax.all_to_all(by_owner, "ctx", split_axis=0, concat_axis=0, tiled=True)
    return moved.reshape(shards * length, channels // shards)


def body(inputs, queries, kv_weight, short_taps, filter_taps, skip_gain, out_weight):
    groups, shards = lax.axis_size("tp"), lax.axis_size("ctx")
    group, core = lax.axis_index("tp"), lax.axis_index("ctx") % 2
    mates = [(d, d ^ 1) for d in range(groups)]
    siblings = [(d, d ^ 1) for d in range(shards)]
    half_rows = out_weight.shape[0] // 2
    part_rows = half_rows // 2
    fetched = [
        lax.ppermute(
            lax.dynamic_slice_in_dim(out_weight, core * half_rows + j * part_rows, part_rows, 0),
            "tp",
            mates,
        )
        for j in range(2)
    ]
    taps_all = to_channels(filter_taps)
    projected = jnp.einsum(
        "td,dkc->tkc", inputs, kv_weight, preferred_element_type=jnp.float32
    ).astype(jnp.bfloat16)
    projected, taps_all = lax.optimization_barrier((projected, taps_all))
    carried = shifted(projected[-2:], "ctx", 1)
    extended = jnp.concatenate([carried, projected], 0).astype(jnp.float32)
    smoothed = (
        short_taps[0] * extended[2:]
        + short_taps[1] * extended[1:-1]
        + short_taps[2] * extended[:-2]
    )
    kv_product = (smoothed[:, 0] * smoothed[:, 1]).astype(jnp.bfloat16)
    kv_product = lax.optimization_barrier(kv_product)
    kv_all = to_channels(kv_product)
    kv_all, fetched[0] = lax.optimization_barrier((kv_all, fetched[0]))
    conv_all = local_conv(kv_all, taps_all)
    conv_all, fetched[1] = lax.optimization_barrier((conv_all, fetched[1]))
    passed = [lax.ppermute(part, "ctx", siblings) for part in fetched]
    mate_weight = jnp.concatenate(fetched + passed, 0)
    channels = conv_all.shape[1]
    rows = queries.shape[0] // groups
    conv_all = conv_all.reshape(shards, groups * rows, channels)
    side = group % 2

    def pair_rows(array, step, dim):
        start = (group - side + step) % groups * rows
        return lax.dynamic_slice_in_dim(array, start, 2 * rows, dim)

    def pair_sum(conv_part, step):
        conv_part = conv_part.reshape(shards * 2 * rows, channels)
        long_conv = lax.all_to_all(conv_part, "ctx", split_axis=0, concat_axis=1, tiled=True)
        gated = (
            pair_rows(queries, step, 0).astype(jnp.float32)
            * (
                long_conv.astype(jnp.float32)
                + skip_gain[None, :] * pair_rows(kv_product, step, 0).astype(jnp.float32)
            )
        ).astype(jnp.bfloat16)
        sent = lax.dynamic_slice_in_dim(gated, (1 - side) * rows, rows, 0)
        sent = jnp.where(
            core == 0, sent, jnp.concatenate([sent[:, half_rows:], sent[:, :half_rows]], 1)
        )
        received = lax.ppermute(sent, "tp", mates)
        own = lax.dynamic_slice_in_dim(gated, side * rows, rows, 0)
        return jnp.dot(own, out_weight, preferred_element_type=jnp.float32) + jnp.dot(
            received, mate_weight, preferred_element_type=jnp.float32
        )

    arrived = []
    for step in range(2, groups, 2):
        part = pair_sum(pair_rows(conv_all, step, 1), step).astype(jnp.bfloat16)
        part, conv_all = lax.optimization_barrier((part, conv_all))
        ring = [(d, (d + step) % groups) for d in range(groups)]
        arrived.append(lax.ppermute(part, "tp", ring))
    total = pair_sum(pair_rows(conv_all, 0, 1), 0)
    total, *arrived = lax.optimization_barrier((total, *arrived))
    for other in arrived:
        total = total + other.astype(jnp.float32)
    return total.astype(jnp.bfloat16)


def solution(mesh):
    return jax.shard_map(
        body,
        mesh=mesh,
        in_specs=(
            P("ctx", None),
            P("ctx", "tp"),
            P(None, None, "tp"),
            P(None, None, "tp"),
            P("ctx", "tp"),
            P("tp"),
            P("tp", None),
        ),
        out_specs=P(("ctx", "tp"), None),
        check_vma=False,
    )
```
